256 devices in a mesh: island: 16 (over y, z_lo), fsdp: 16 (over x, z_hi, core).
Axes of the slice: x: 4, y: 4, z: 8 (z_hi: 2, z_lo: 4; z = z_hi * 4 + z_lo), core: 2. Of those that a mesh axis runs over, the one named last changes fastest.
Arguments:
- local_weights: bfloat16 [16, 8, 8192, 1024], P('island', None, 'fsdp'), may hold values from -6 to 6
- master: float32 [8, 8192, 1024], P(None, ('fsdp', 'island')), may hold values from -6 to 6
- momentum: float32 [8, 8192, 1024], P(None, ('fsdp', 'island')), may hold values from -4 to 4
Outputs:
- fresh_weights: bfloat16 [8, 8192, 1024], P(None, 'fsdp')
- new_master: float32 [8, 8192, 1024], P(None, ('fsdp', 'island'))
- new_momentum: float32 [8, 8192, 1024], P(None, ('fsdp', 'island'))
The draws below stay inside these ranges and needn't reach their ends.
All inputs are finite; a program needn't handle non-finite values.
Results may differ from the reference program's by a relative error of at most 0.015.
Values may be sent and summed in bfloat16 or wider, within the bound.
No kernel may reach another device: no remote copies, remote signals or barrier semaphores. Data moves between devices by JAX's collectives and lax.ppermute only.
A program may use at most 128 MiB of HBM per device.

```python
import jax
import jax.numpy as jnp

D = 8192
KVW = 1024
PROJ = 8
ISLANDS = 16
N_ISLAND = 16


def block_scale(own_key, extent, split, low, high):
    def one(axis_at, shards_of):
        draws = jax.random.uniform(jax.random.fold_in(jax.random.fold_in(own_key, 6), axis_at), (shards_of,), jnp.float32, low / len(split), high / len(split))
        return jnp.repeat(jnp.exp(draws), extent[axis_at] // shards_of).reshape((-1,) + (1,) * (len(extent) - axis_at - 1))

    gain = one(*split[0])
    for cut in split[1:]:
        gain = gain * one(*cut)
    return gain


def centred(own_key, dims, spread, most, cuts=(), held_as=jnp.bfloat16):
    array = spread * jax.random.normal(own_key, dims, jnp.float32)
    if cuts:
        array = array * block_scale(own_key, dims, cuts, -0.22, 0.18)
    return jnp.clip(array, -most, most).astype(held_as)


def setup_inputs(seed: int = 0) -> dict:
    keys = jax.random.split(jax.random.key(seed), 4)
    return {
        "local_weights": centred(keys[0], (ISLANDS, PROJ, D, KVW), 1.0, 6.0, ((0, 16), (2, 16))),
        "master": centred(keys[1], (PROJ, D, KVW), 1.0, 6.0, ((1, 256),), jnp.float32),
        "momentum": centred(keys[2], (PROJ, D, KVW), 0.5, 4.0, ((1, 256),), jnp.float32),
    }


outer_rate = 0.7
outer_mu = 0.9


def reference(local_weights, master, momentum):
    averaged = jnp.sum(local_weights.astype(jnp.float32), axis=0) / N_ISLAND
    pseudo = master - averaged
    new_momentum = outer_mu * momentum + pseudo
    new_master = master - outer_rate * (pseudo + outer_mu * new_momentum)
    fresh_weights = new_master.astype(jnp.bfloat16)
    return (fresh_weights, new_master, new_momentum)
```

```python
import jax
import jax.numpy as jnp
from jax import lax
from jax.sharding import Mesh, PartitionSpec as P

RATE = 0.7
MU = 0.9
NY = 4
NZ = 4
CHUNKS = 4
F32 = jnp.float32
BF16 = jnp.bfloat16


def shift(a, s):
    return lax.ppermute(a, "y", [(i, (i + s) % NY) for i in range(NY)])


def swap(a, k):
    return lax.ppermute(a, "z", [(i, i ^ k) for i in range(NZ)])


def rows(a, block, n):
    return lax.dynamic_slice_in_dim(a, block * n, n, axis=1)


def chunk_step(x, master, momentum, y, z):
    n = x.shape[1] // NY
    h = x.shape[0] // 2
    m = n // NZ
    far = rows(x, (y + 2) % NY, n)
    up = rows(x, (y + 1) % NY, n)
    down = rows(x, (y + 3) % NY, n)
    own = rows(x, y, n)
    from_below = shift(far[h:], 1)
    from_above = shift(far[:h], -1)
    up = jnp.concatenate([up[:h], (up[h:].astype(F32) + from_below.astype(F32)).astype(BF16)])
    down = jnp.concatenate([(down[:h].astype(F32) + from_above.astype(F32)).astype(BF16), down[h:]])
    got_up = shift(up, 1)
    got_down = shift(down, -1)
    part = own.astype(F32) + got_up.astype(F32) + got_down.astype(F32)
    partb = part.astype(BF16)
    got = [swap(rows(partb, z ^ k, m), k) for k in (1, 2, 3)]
    total = rows(part, z, m) + (got[0].astype(F32) + got[1].astype(F32) + got[2].astype(F32))
    pseudo = master - total / 16
    new_momentum = MU * momentum + pseudo
    new_master = master - RATE * (pseudo + MU * new_momentum)
    fresh = new_master.astype(BF16)
    block = jnp.zeros((x.shape[0], n, x.shape[2]), BF16)
    block = lax.dynamic_update_slice_in_dim(block, fresh, z * m, 1)
    for k in (1, 2, 3):
        block = lax.dynamic_update_slice_in_dim(block, swap(fresh, k), (z ^ k) * m, 1)
    below = shift(block, 1)
    above = shift(block, -1)
    far0 = shift(below[:h], 1)
    far1 = shift(above[h:], -1)
    return new_master, new_momentum, (block, below, above, far0, far1)


def on_device(x, master, momentum):
    y, z = lax.axis_index("y"), lax.axis_index("z")
    x = x[0]
    p = x.shape[0] // CHUNKS
    n = x.shape[1] // NY
    h = p // 2
    out = jnp.zeros(x.shape, BF16)
    nm, nv = [], []
    for c in range(CHUNKS):
        s = slice(c * p, (c + 1) * p)
        a, b, (block, below, above, far0, far1) = chunk_step(x[s], master[s], momentum[s], y, z)
        nm.append(a)
        nv.append(b)
        for q, d, o in ((block, 0, 0), (below, 3, 0), (above, 1, 0), (far0, 2, 0), (far1, 2, h)):
            out = lax.dynamic_update_slice(out, q, (c * p + o, (y + d) % NY * n, 0))
    return out, jnp.concatenate(nm), jnp.concatenate(nv)


def solution(mesh):
    names = mesh.axis_names
    assert names == ("island", "fsdp")
    fine = Mesh(mesh.devices.reshape(NY, NZ, -1), ("y", "z", "fsdp"))
    owned = P(None, ("fsdp", "y", "z"), None)
    return jax.shard_map(
        on_device,
        mesh=fine,
        in_specs=(P(("y", "z"), None, "fsdp", None), owned, owned),
        out_specs=(P(None, "fsdp", None), owned, owned),
        check_vma=False,
    )
```

```python
import functools

import jax
import jax.numpy as jnp
from jax import lax
from jax.experimental import pallas as pl
from jax.experimental.pallas import tpu as pltpu
from jax.sharding import Mesh, PartitionSpec as P

RATE = 0.7
MU = 0.9
NY = 4
NZ = 4
CHUNKS = 4
F32 = jnp.float32
BF16 = jnp.bfloat16
ANY = pl.BlockSpec(memory_space=pl.ANY)
HBM = pl.BlockSpec(memory_space=pltpu.HBM)
ROWS = 32
VMEM = 16 << 20


def shift(a, s):
    return lax.ppermute(a, "y", [(i, (i + s) % NY) for i in range(NY)])


def swap(a, k):
    return lax.ppermute(a, "z", [(i, i ^ k) for i in range(NZ)])


def ds(block, n):
    return pl.ds(pl.multiple_of(block * n, n), n)


def move(*copies):
    started = [pltpu.make_async_copy(*c) for c in copies]
    for c in started:
        c.start()
    for c in started:
        c.wait()


class Steps:
    def __init__(self, x, master, momentum, where):
        self.x, self.master, self.momentum, self.where = x, master, momentum, where
        _, self.projs, rows, self.w = x.shape
        self.p = self.projs // CHUNKS
        self.h = self.p // 2
        self.n = rows // NY
        self.m = self.n // NZ
        self.last = None
        self.out, self.new_master, self.new_momentum = None, {}, {}

    def call(self, body, ins, outs, alias=(), scratch=()):
        arrays = [a for a, _ in ins]
        specs = [s for _, s in ins]
        n_in, n_out = len(arrays), len(outs)
        aliases = {}
        for array, k in alias:
            if array is not None:
                aliases[1 + len(arrays)] = k
                arrays.append(array)
                specs.append(outs[k][2])
        if self.last is not None:
            arrays.append(self.last)
            specs.append(ANY)
        total = len(arrays)

        def kernel(where, *refs):
            body(where, *refs[:n_in], *refs[total:])

        got = pl.pallas_call(
            kernel,
            out_shape=[jax.ShapeDtypeStruct(s, t) for s, t, _ in outs],
            grid_spec=pltpu.PrefetchScalarGridSpec(
                num_scalar_prefetch=1,
                grid=(1,),
                in_specs=specs,
                out_specs=[s for _, _, s in outs],
                scratch_shapes=scratch,
            ),
            input_output_aliases=aliases,
            compiler_params=pltpu.CompilerParams(vmem_limit_bytes=VMEM),
            cost_estimate=pl.CostEstimate(flops=1000, bytes_accessed=1000, transcendentals=0),
        )(self.where, *arrays)
        if len(got) > 1:
            self.last = got[-1]
        return got

    def full(self, shape):
        return pl.BlockSpec(shape, lambda i, w: (0,) * len(shape))

    def of_x(self, where, c, d, first, count):
        return (0, pl.ds(c * self.p + first, count), ds((where[0] + d) % NY, self.n))

    def of_out(self, where, c, d, first, count):
        return (pl.ds(c * self.p + first, count), ds((where[0] + d) % NY, self.n))

    def first(self, c):
        p, h, n, w = self.p, self.h, self.n, self.w

        def body(where, x, up, down, sems):
            move(
                (x.at[self.of_x(where, c, 2, h, h)], up, sems.at[0]),
                (x.at[self.of_x(where, c, 2, 0, h)], down, sems.at[1]),
            )

        up, down = self.call(body, [(self.x, HBM)], [((h, n, w), BF16, ANY)] * 2, scratch=[pltpu.SemaphoreType.DMA((2,))])
        return shift(up, 1), shift(down, -1)

    def second(self, c, got):
        p, h, n, w = self.p, self.h, self.n, self.w

        def body(where, x, below, above, up, down, sems):
            move(
                (x.at[self.of_x(where, c, 1, 0, p)], up, sems.at[0]),
                (x.at[self.of_x(where, c, 3, 0, p)], down, sems.at[1]),
            )

            @pl.loop(0, n // ROWS)
            def _(i):
                r = ds(i, ROWS)
                up[h:, r] = (up[h:, r].astype(F32) + below[:, r].astype(F32)).astype(BF16)
                down[:h, r] = (down[:h, r].astype(F32) + above[:, r].astype(F32)).astype(BF16)

        up, down = self.call(
            body,
            [(self.x, HBM), (got[0], self.full((h, n, w))), (got[1], self.full((h, n, w)))],
            [((p, n, w), BF16, self.full((p, n, w)))] * 2,
            scratch=[pltpu.SemaphoreType.DMA((2,))],
        )
        return shift(up, 1), shift(down, -1)

    def third(self, c, got):
        p, n, m, w = self.p, self.n, self.m, self.w

        def body(where, x, below, above, keep, send, own, sems):
            move((x.at[self.of_x(where, c, 0, 0, p)], own, sems.at[0]))
            z = where[1]
            for out, at, k in ((keep, 0, 0), (keep, m, 3), (send, 0, 1), (send, m, 2)):
                r = ds(z ^ k, m)
                t = own[:, r].astype(F32) + below[:, r].astype(F32) + above[:, r].astype(F32)
                out[:, at : at + m] = t.astype(out.dtype)

        keep, send = self.call(
            body,
            [(self.x, HBM), (got[0], self.full((p, n, w))), (got[1], self.full((p, n, w)))],
            [
                ((p, 2 * m, w), F32, self.full((p, 2 * m, w))),
                ((p, 2 * m, w), BF16, self.full((p, 2 * m, w))),
            ],
            scratch=[pltpu.VMEM((p, n, w), BF16), pltpu.SemaphoreType.DMA((1,))],
        )
        return keep, swap(send, 1)

    def fourth(self, c, got):
        p, m, w = self.p, self.m, self.w

        def body(where, kept, came, keep, send):
            keep[...] = kept[:, :m] + came[:, :m].astype(F32)
            send[...] = (kept[:, m:] + came[:, m:].astype(F32)).astype(BF16)

        keep, send = self.call(
            body,
            [(a, self.full((p, 2 * m, w))) for a in got],
            [((p, m, w), F32, self.full((p, m, w))), ((p, m, w), BF16, self.full((p, m, w)))],
        )
        return keep, swap(send, 3)

    def update(self, c, got):
        p, m, w = self.p, self.m, self.w
        mine = pl.BlockSpec((p, m, w), lambda i, w_: (c, 0, 0))

        def body(where, kept, came, master, momentum, new_master, new_momentum, fresh):
            pseudo = master[...] - (kept[...] + came[...].astype(F32)) / 16
            nv = MU * momentum[...] + pseudo
            nm = master[...] - RATE * (pseudo + MU * nv)
            new_master[...] = nm
            new_momentum[...] = nv
            fresh[...] = nm.astype(BF16)

        nm, nv, fresh = self.call(
            body,
            [(a, self.full((p, m, w))) for a in got] + [(self.master, mine), (self.momentum, mine)],
            [
                ((p, m, w), F32, self.full((p, m, w))),
                ((p, m, w), F32, self.full((p, m, w))),
                ((p, m, w), BF16, self.full((p, m, w))),
            ],
        )
        self.new_master[c], self.new_momentum[c] = nm, nv
        return fresh, swap(fresh, 3)

    def pair(self, c, got):
        p, m, w = self.p, self.m, self.w

        def body(where, mine, came, both, mark):
            both[:, :m] = mine[...]
            both[:, m:] = came[...]

        both, _ = self.call(
            body,
            [(a, self.full((p, m, w))) for a in got],
            [((p, 2 * m, w), BF16, self.full((p, 2 * m, w))), ((8, 128), F32, self.full((8, 128)))],
        )
        return both, swap(both, 1)

    def whole(self, c, got):
        p, n, m, w = self.p, self.n, self.m, self.w

        def body(where, mine, came, out, block, sems):
            z = where[1]
            for src, at, k in ((mine, 0, 0), (mine, m, 3), (came, 0, 1), (came, m, 2)):
                block[:, ds(z ^ k, m)] = src[:, at : at + m]
            move((block, out.at[self.of_out(where, c, 0, 0, p)], sems.at[0]))

        self.out, block = self.call(
            body,
            [(a, self.full((p, 2 * m, w))) for a in got],
            [((self.projs, NY * n, w), BF16, HBM), ((p, n, w), BF16, self.full((p, n, w)))],
            alias=[(self.out, 0)],
            scratch=[pltpu.SemaphoreType.DMA((1,))],
        )
        return shift(block, 1), shift(block, -1)

    def pass_on(self, c, got):
        p, h, n, w = self.p, self.h, self.n, self.w

        def body(where, below, above, out, up, down, sems):
            move(
                (below.at[pl.ds(0, h)], up, sems.at[0]),
                (above.at[pl.ds(h, h)], down, sems.at[1]),
                (below, out.at[self.of_out(where, c, 3, 0, p)], sems.at[2]),
                (above, out.at[self.of_out(where, c, 1, 0, p)], sems.at[3]),
            )

        self.out, up, down = self.call(
            body,
            [(a, ANY) for a in got],
            [(self.out.shape, BF16, HBM), ((h, n, w), BF16, ANY), ((h, n, w), BF16, ANY)],
            alias=[(self.out, 0)],
            scratch=[pltpu.SemaphoreType.DMA((4,))],
        )
        return shift(up, 1), shift(down, -1)

    def finish(self, c, got):
        p, h, n, w = self.p, self.h, self.n, self.w

        def body(where, low, high, out, sems):
            move(
                (low, out.at[self.of_out(where, c, 2, 0, h)], sems.at[0]),
                (high, out.at[self.of_out(where, c, 2, h, h)], sems.at[1]),
            )

        (self.out,) = self.call(
            body,
            [(a, ANY) for a in got],
            [(self.out.shape, BF16, HBM)],
            alias=[(self.out, 0)],
            scratch=[pltpu.SemaphoreType.DMA((2,))],
        )


PLAN = "a0 a1 m0 a2 m1 s0 a3 h0 m2 s1 u0 h1 p0 m3 s2 u1 g0 h2 p1 s3 u2 h3 g1 p2 u3 o0 g2 p3 o1 f0 g3 o2 f1 o3 f2 f3"


def on_device(x, master, momentum):
    where = jnp.stack([lax.axis_index("y"), lax.axis_index("z")]).astype(jnp.int32)
    s = Steps(x, master, momentum, where)
    held = [None] * CHUNKS
    kinds = dict(a=None, m=s.second, s=s.third, h=s.fourth, u=s.update, p=s.pair, g=s.whole, o=s.pass_on, f=s.finish)
    for step in PLAN.split():
        c = int(step[1:])
        held[c] = s.first(c) if step[0] == "a" else kinds[step[0]](c, held[c])
    join = lambda d: jnp.concatenate([d[c] for c in range(CHUNKS)])
    return s.out, join(s.new_master), join(s.new_momentum)


def solution(mesh):
    fine = Mesh(mesh.devices.reshape(NY, NZ, -1), ("y", "z", "fsdp"))
    owned = P(None, ("fsdp", "y", "z"), None)
    return jax.shard_map(
        on_device,
        mesh=fine,
        in_specs=(P(("y", "z"), None, "fsdp", None), owned, owned),
        out_specs=(P(None, "fsdp", None), owned, owned),
        check_vma=False,
    )
```

```python
import functools

import jax
import jax.numpy as jnp
from jax import lax
from jax.experimental import pallas as pl
from jax.experimental.pallas import tpu as pltpu
from jax.sharding import Mesh, PartitionSpec as P

RATE = 0.7
MU = 0.9
NY = 4
NZ = 4
CHUNKS = 4
F32 = jnp.float32
BF16 = jnp.bfloat16
ANY = pl.BlockSpec(memory_space=pl.ANY)
HBM = pl.BlockSpec(memory_space=pltpu.HBM)
ROWS = 32
VMEM = 16 << 20


def shift(a, s):
    return lax.ppermute(a, "y", [(i, (i + s) % NY) for i in range(NY)])


def swap(a, k):
    return lax.ppermute(a, "z", [(i, i ^ k) for i in range(NZ)])


def ds(block, n):
    return pl.ds(pl.multiple_of(block * n, n), n)


def move(*copies):
    started = [pltpu.make_async_copy(*c) for c in copies]
    for c in started:
        c.start()
    for c in started:
        c.wait()


class Steps:
    def __init__(self, x, master, momentum, where):
        self.x, self.master, self.momentum, self.where = x, master, momentum, where
        _, self.projs, rows, self.w = x.shape
        self.p = self.projs // CHUNKS
        self.h = self.p // 2
        self.n = rows // NY
        self.m = self.n // NZ
        self.last = None
        self.out, self.new_master, self.new_momentum = None, {}, {}

    def call(self, body, ins, outs, alias=(), scratch=()):
        arrays = [a for a, _ in ins]
        specs = [s for _, s in ins]
        n_in, n_out = len(arrays), len(outs)
        aliases = {}
        for array, k in alias:
            if array is not None:
                aliases[1 + len(arrays)] = k
                arrays.append(array)
                specs.append(outs[k][2])
        if self.last is not None:
            arrays.append(self.last)
            specs.append(ANY)
        total = len(arrays)

        def kernel(where, *refs):
            body(where, *refs[:n_in], *refs[total:])

        got = pl.pallas_call(
            kernel,
            out_shape=[jax.ShapeDtypeStruct(s, t) for s, t, _ in outs],
            grid_spec=pltpu.PrefetchScalarGridSpec(
                num_scalar_prefetch=1,
                grid=(1,),
                in_specs=specs,
                out_specs=[s for _, _, s in outs],
                scratch_shapes=scratch,
            ),
            input_output_aliases=aliases,
            compiler_params=pltpu.CompilerParams(vmem_limit_bytes=VMEM),
            cost_estimate=pl.CostEstimate(flops=1000, bytes_accessed=1000, transcendentals=0),
        )(self.where, *arrays)
        if len(got) > 1:
            self.last = got[-1]
        return got

    def full(self, shape):
        return pl.BlockSpec(shape, lambda i, w: (0,) * len(shape))

    def of_x(self, where, c, d, first, count):
        return (0, pl.ds(c * self.p + first, count), ds((where[0] + d) % NY, self.n))

    def of_out(self, where, c, d, first, count):
        return (pl.ds(c * self.p + first, count), ds((where[0] + d) % NY, self.n))

    def first(self, c):
        p, h, n, w = self.p, self.h, self.n, self.w
        if self.last is None:
            block = (self.where[0] + 2) % NY * n
            far = [lax.dynamic_slice(self.x, (0, e * p, block, 0), (1, p, n, w))[0] for e in (c, c + 1)]
            up = jnp.concatenate([t[h:] for t in far])
            down = jnp.concatenate([t[:h] for t in far])
            self.last = up
            return shift(up, 1), shift(down, -1)

        def body(where, x, up, down, sems):
            move(
                (x.at[self.of_x(where, c, 2, h, h)], up.at[pl.ds(0, h)], sems.at[0]),
                (x.at[self.of_x(where, c + 1, 2, h, h)], up.at[pl.ds(h, h)], sems.at[1]),
                (x.at[self.of_x(where, c, 2, 0, h)], down.at[pl.ds(0, h)], sems.at[2]),
                (x.at[self.of_x(where, c + 1, 2, 0, h)], down.at[pl.ds(h, h)], sems.at[3]),
            )

        up, down = self.call(
            body,
            [(self.x, HBM)],
            [((2 * h, n, w), BF16, ANY)] * 2,
            scratch=[pltpu.SemaphoreType.DMA((4,))],
        )
        return shift(up, 1), shift(down, -1)

    def second(self, c, got):
        p, h, n, w = self.p, self.h, self.n, self.w
        half = pl.BlockSpec((h, n, w), lambda i, w_: (c % 2, 0, 0))

        def body(where, x, below, above, up, down, sems):
            move(
                (x.at[self.of_x(where, c, 1, 0, p)], up, sems.at[0]),
                (x.at[self.of_x(where, c, 3, 0, p)], down, sems.at[1]),
            )

            @pl.loop(0, n // ROWS)
            def _(i):
                r = ds(i, ROWS)
                up[h:, r] = (up[h:, r].astype(F32) + below[:, r].astype(F32)).astype(BF16)
                down[:h, r] = (down[:h, r].astype(F32) + above[:, r].astype(F32)).astype(BF16)

        up, down = self.call(
            body,
            [(self.x, HBM), (got[0], half), (got[1], half)],
            [((p, n, w), BF16, self.full((p, n, w)))] * 2,
            scratch=[pltpu.SemaphoreType.DMA((2,))],
        )
        return shift(up, 1), shift(down, -1)

    def third(self, c, got):
        p, n, m, w = self.p, self.n, self.m, self.w

        def body(where, x, below, above, keep, send, own, sems):
            move((x.at[self.of_x(where, c, 0, 0, p)], own, sems.at[0]))
            z = where[1]
            for out, at, k in ((keep, 0, 0), (keep, m, 3), (send, 0, 1), (send, m, 2)):
                r = ds(z ^ k, m)
                t = own[:, r].astype(F32) + below[:, r].astype(F32) + above[:, r].astype(F32)
                out[:, at : at + m] = t.astype(out.dtype)

        keep, send = self.call(
            body,
            [(self.x, HBM), (got[0], self.full((p, n, w))), (got[1], self.full((p, n, w)))],
            [
                ((p, 2 * m, w), F32, self.full((p, 2 * m, w))),
                ((p, 2 * m, w), BF16, self.full((p, 2 * m, w))),
            ],
            scratch=[pltpu.VMEM((p, n, w), BF16), pltpu.SemaphoreType.DMA((1,))],
        )
        return keep, swap(send, 1)

    def fourth(self, c, got):
        p, m, w = self.p, self.m, self.w

        def body(where, kept, came, keep, send):
            keep[...] = kept[:, :m] + came[:, :m].astype(F32)
            send[...] = (kept[:, m:] + came[:, m:].astype(F32)).astype(BF16)

        keep, send = self.call(
            body,
            [(a, self.full((p, 2 * m, w))) for a in got],
            [((p, m, w), F32, self.full((p, m, w))), ((p, m, w), BF16, self.full((p, m, w)))],
        )
        return keep, swap(send, 3)

    def update(self, c, got):
        p, m, w = self.p, self.m, self.w
        mine = pl.BlockSpec((p, m, w), lambda i, w_: (c, 0, 0))

        def body(where, kept, came, master, momentum, new_master, new_momentum, fresh):
            pseudo = master[...] - (kept[...] + came[...].astype(F32)) / 16
            nv = MU * momentum[...] + pseudo
            nm = master[...] - RATE * (pseudo + MU * nv)
            new_master[...] = nm
            new_momentum[...] = nv
            fresh[...] = nm.astype(BF16)

        nm, nv, fresh = self.call(
            body,
            [(a, self.full((p, m, w))) for a in got] + [(self.master, mine), (self.momentum, mine)],
            [
                ((p, m, w), F32, self.full((p, m, w))),
                ((p, m, w), F32, self.full((p, m, w))),
                ((p, m, w), BF16, self.full((p, m, w))),
            ],
        )
        self.new_master[c], self.new_momentum[c] = nm, nv
        return fresh, swap(fresh, 3)

    def pair(self, c, got):
        p, m, w = self.p, self.m, self.w

        def body(where, mine, came, both, mark):
            both[:, :m] = mine[...]
            both[:, m:] = came[...]

        both, _ = self.call(
            body,
            [(a, self.full((p, m, w))) for a in got],
            [((p, 2 * m, w), BF16, self.full((p, 2 * m, w))), ((8, 128), F32, self.full((8, 128)))],
        )
        return both, swap(both, 1)

    def whole(self, c, got):
        p, n, m, w = self.p, self.n, self.m, self.w

        def body(where, mine, came, out, block, sems):
            z = where[1]
            for src, at, k in ((mine, 0, 0), (mine, m, 3), (came, 0, 1), (came, m, 2)):
                block[:, ds(z ^ k, m)] = src[:, at : at + m]
            move((block, out.at[self.of_out(where, c, 0, 0, p)], sems.at[0]))

        self.out, block = self.call(
            body,
            [(a, self.full((p, 2 * m, w))) for a in got],
            [((self.projs, NY * n, w), BF16, HBM), ((p, n, w), BF16, self.full((p, n, w)))],
            alias=[(self.out, 0)],
            scratch=[pltpu.SemaphoreType.DMA((1,))],
        )
        return shift(block, 1), shift(block, -1)

    def pass_on(self, c, got):
        p, h, n, w = self.p, self.h, self.n, self.w
        many = len(got) // 2

        def body(where, *refs):
            came, (out, up, down, sems) = refs[: 2 * many], refs[2 * many :]
            copies = []
            for j in range(many):
                below, above = came[2 * j], came[2 * j + 1]
                copies += [
                    (below.at[pl.ds(0, h)], up.at[pl.ds(j * h, h)], sems.at[4 * j]),
                    (above.at[pl.ds(h, h)], down.at[pl.ds(j * h, h)], sems.at[4 * j + 1]),
                    (below, out.at[self.of_out(where, c + j, 3, 0, p)], sems.at[4 * j + 2]),
                    (above, out.at[self.of_out(where, c + j, 1, 0, p)], sems.at[4 * j + 3]),
                ]
            move(*copies)

        self.out, up, down = self.call(
            body,
            [(a, ANY) for a in got],
            [(self.out.shape, BF16, HBM)] + [((many * h, n, w), BF16, ANY)] * 2,
            alias=[(self.out, 0)],
            scratch=[pltpu.SemaphoreType.DMA((4 * many,))],
        )
        return shift(up, 1), shift(down, -1)

    def finish(self, c, got):
        h = self.h
        many = got[0].shape[0] // h

        def body(where, low, high, out, sems):
            copies = []
            for j in range(many):
                r = pl.ds(j * h, h)
                copies += [
                    (low.at[r], out.at[self.of_out(where, c + j, 2, 0, h)], sems.at[2 * j]),
                    (high.at[r], out.at[self.of_out(where, c + j, 2, h, h)], sems.at[2 * j + 1]),
                ]
            move(*copies)

        (self.out,) = self.call(
            body,
            [(a, ANY) for a in got],
            [(self.out.shape, BF16, HBM)],
            alias=[(self.out, 0)],
            scratch=[pltpu.SemaphoreType.DMA((2 * many,))],
        )


PLAN = (
    "a0", "a2", "m0", "m1", "m2", "s0", "h0", "s1", "u0", "p0",
    "h1", "s2", "m3", "u1", "h2", "p1", "g0", "u2", "s3", "g1",
    "p2", "h3", "g2", "o0", "u3", "p3", "f0", "g3", "o2", "o3",
    "f2", "f3",
)


def on_device(x, master, momentum):
    where = jnp.stack([lax.axis_index("y"), lax.axis_index("z")]).astype(jnp.int32)
    s = Steps(x, master, momentum, where)
    held = [None] * CHUNKS
    kinds = dict(a=None, m=s.second, s=s.third, h=s.fourth, u=s.update, p=s.pair, g=s.whole, o=s.pass_on, f=s.finish)
    for step in PLAN:
        c = int(step[1:])
        if step[0] == "a":
            held[c] = held[c + 1] = s.first(c)
        elif step == "o0":
            held[c] = s.pass_on(c, held[c] + held[c + 1])
        else:
            held[c] = kinds[step[0]](c, held[c])
    join = lambda d: jnp.concatenate([d[c] for c in range(CHUNKS)])
    return s.out, join(s.new_master), join(s.new_momentum)


def solution(mesh):
    fine = Mesh(mesh.devices.reshape(NY, NZ, -1), ("y", "z", "fsdp"))
    owned = P(None, ("fsdp", "y", "z"), None)
    return jax.shard_map(
        on_device,
        mesh=fine,
        in_specs=(P(("y", "z"), None, "fsdp", None), owned, owned),
        out_specs=(P(None, "fsdp", None), owned, owned),
        check_vma=False,
    )
```

```python
import functools

import jax
import jax.numpy as jnp
from jax import lax
from jax.experimental import pallas as pl
from jax.experimental.pallas import tpu as pltpu
from jax.sharding import Mesh, PartitionSpec as P

RATE = 0.7
MU = 0.9
NY = 4
NZ = 4
CHUNKS = 4
F32 = jnp.float32
BF16 = jnp.bfloat16
ANY = pl.BlockSpec(memory_space=pl.ANY)
HBM = pl.BlockSpec(memory_space=pltpu.HBM)
ROWS = 32
VMEM = 16 << 20


def shift(a, s):
    return lax.ppermute(a, "y", [(i, (i + s) % NY) for i in range(NY)])


def swap(a, k):
    return lax.ppermute(a, "z", [(i, i ^ k) for i in range(NZ)])


def ds(block, n):
    return pl.ds(pl.multiple_of(block * n, n), n)


def move(*copies):
    started = [pltpu.make_async_copy(*c) for c in copies]
    for c in started:
        c.start()
    for c in started:
        c.wait()


class Steps:
    def __init__(self, x, master, momentum, where):
        self.x, self.master, self.momentum, self.where = x, master, momentum, where
        _, self.projs, rows, self.w = x.shape
        self.p = self.projs // CHUNKS
        self.h = self.p // 2
        self.n = rows // NY
        self.m = self.n // NZ
        self.last = None
        self.out, self.new_master, self.new_momentum = None, {}, {}

    def call(self, body, ins, outs, alias=(), scratch=()):
        arrays = [a for a, _ in ins]
        specs = [s for _, s in ins]
        n_in, n_out = len(arrays), len(outs)
        aliases = {}
        for array, k in alias:
            if array is not None:
                aliases[1 + len(arrays)] = k
                arrays.append(array)
                specs.append(outs[k][2])
        if self.last is not None:
            arrays.append(self.last)
            specs.append(ANY)
        total = len(arrays)

        def kernel(where, *refs):
            body(where, *refs[:n_in], *refs[total:])

        got = pl.pallas_call(
            kernel,
            out_shape=[jax.ShapeDtypeStruct(s, t) for s, t, _ in outs],
            grid_spec=pltpu.PrefetchScalarGridSpec(
                num_scalar_prefetch=1,
                grid=(1,),
                in_specs=specs,
                out_specs=[s for _, _, s in outs],
                scratch_shapes=scratch,
            ),
            input_output_aliases=aliases,
            compiler_params=pltpu.CompilerParams(vmem_limit_bytes=VMEM),
            cost_estimate=pl.CostEstimate(flops=1000, bytes_accessed=1000, transcendentals=0),
        )(self.where, *arrays)
        if len(got) > 1:
            self.last = got[-1]
        return got

    def full(self, shape):
        return pl.BlockSpec(shape, lambda i, w: (0,) * len(shape))

    def of_x(self, where, c, d, first, count):
        return (0, pl.ds(c * self.p + first, count), ds((where[0] + d) % NY, self.n))

    def of_out(self, where, c, d, first, count):
        return (pl.ds(c * self.p + first, count), ds((where[0] + d) % NY, self.n))

    def first(self, c, many):
        p, h, n, w = self.p, self.h, self.n, self.w
        if self.last is None:
            block = (self.where[0] + 2) % NY * n
            far = [lax.dynamic_slice(self.x, (0, (c + j) * p, block, 0), (1, p, n, w))[0] for j in range(many)]
            self.last = up = jnp.concatenate([t[h:] for t in far])
            return shift(up, 1), shift(jnp.concatenate([t[:h] for t in far]), -1)

        def body(where, x, up, down, sems):
            copies = []
            for j in range(many):
                r = pl.ds(j * h, h)
                copies += [
                    (x.at[self.of_x(where, c + j, 2, h, h)], up.at[r], sems.at[2 * j]),
                    (x.at[self.of_x(where, c + j, 2, 0, h)], down.at[r], sems.at[2 * j + 1]),
                ]
            move(*copies)

        up, down = self.call(
            body,
            [(self.x, HBM)],
            [((many * h, n, w), BF16, ANY)] * 2,
            scratch=[pltpu.SemaphoreType.DMA((2 * many,))],
        )
        return shift(up, 1), shift(down, -1)

    def second(self, c, many, got, j):
        p, h, n, w = self.p, self.h, self.n, self.w
        part = pl.BlockSpec((many * h, n, w), lambda i, w_: (j // many, 0, 0))

        def body(where, x, below, above, up, down, sems):
            move(
                (x.at[self.of_x(where, c, 1, 0, many * p)], up, sems.at[0]),
                (x.at[self.of_x(where, c, 3, 0, many * p)], down, sems.at[1]),
            )

            @pl.loop(0, n // ROWS)
            def _(i):
                r = ds(i, ROWS)
                for k in range(many):
                    came, low, high = pl.ds(k * h, h), pl.ds(k * p, h), pl.ds(k * p + h, h)
                    up[high, r] = (up[high, r].astype(F32) + below[came, r].astype(F32)).astype(BF16)
                    down[low, r] = (down[low, r].astype(F32) + above[came, r].astype(F32)).astype(BF16)

        up, down = self.call(
            body,
            [(self.x, HBM), (got[0], part), (got[1], part)],
            [((many * p, n, w), BF16, self.full((many * p, n, w)))] * 2,
            scratch=[pltpu.SemaphoreType.DMA((2,))],
        )
        return shift(up, 1), shift(down, -1)

    def third(self, c, got, j):
        p, n, m, w = self.p, self.n, self.m, self.w
        part = pl.BlockSpec((p, n, w), lambda i, w_: (j, 0, 0))

        def body(where, x, below, above, keep, send, own, sems):
            move((x.at[self.of_x(where, c, 0, 0, p)], own, sems.at[0]))
            z = where[1]
            for out, at, k in ((keep, 0, 0), (keep, m, 3), (send, 0, 1), (send, m, 2)):
                r = ds(z ^ k, m)
                t = own[:, r].astype(F32) + below[:, r].astype(F32) + above[:, r].astype(F32)
                out[:, at : at + m] = t.astype(out.dtype)

        keep, send = self.call(
            body,
            [(self.x, HBM), (got[0], part), (got[1], part)],
            [
                ((p, 2 * m, w), F32, self.full((p, 2 * m, w))),
                ((p, 2 * m, w), BF16, self.full((p, 2 * m, w))),
            ],
            scratch=[pltpu.VMEM((p, n, w), BF16), pltpu.SemaphoreType.DMA((1,))],
        )
        return keep, swap(send, 1)

    def fourth(self, c, got):
        p, m, w = self.p, self.m, self.w

        def body(where, kept, came, keep, send):
            keep[...] = kept[:, :m] + came[:, :m].astype(F32)
            send[...] = (kept[:, m:] + came[:, m:].astype(F32)).astype(BF16)

        keep, send = self.call(
            body,
            [(a, self.full((p, 2 * m, w))) for a in got],
            [((p, m, w), F32, self.full((p, m, w))), ((p, m, w), BF16, self.full((p, m, w)))],
        )
        return keep, swap(send, 3)

    def update(self, c, got):
        p, m, w = self.p, self.m, self.w
        mine = pl.BlockSpec((p, m, w), lambda i, w_: (c, 0, 0))

        def body(where, kept, came, master, momentum, new_master, new_momentum, fresh):
            pseudo = master[...] - (kept[...] + came[...].astype(F32)) / 16
            nv = MU * momentum[...] + pseudo
            nm = master[...] - RATE * (pseudo + MU * nv)
            new_master[...] = nm
            new_momentum[...] = nv
            fresh[...] = nm.astype(BF16)

        nm, nv, fresh = self.call(
            body,
            [(a, self.full((p, m, w))) for a in got] + [(self.master, mine), (self.momentum, mine)],
            [
                ((p, m, w), F32, self.full((p, m, w))),
                ((p, m, w), F32, self.full((p, m, w))),
                ((p, m, w), BF16, self.full((p, m, w))),
            ],
        )
        self.new_master[c], self.new_momentum[c] = nm, nv
        return fresh, swap(fresh, 3)

    def pair(self, c, got):
        p, m, w = self.p, self.m, self.w

        def body(where, mine, came, both, mark):
            both[:, :m] = mine[...]
            both[:, m:] = came[...]

        both, _ = self.call(
            body,
            [(a, self.full((p, m, w))) for a in got],
            [((p, 2 * m, w), BF16, self.full((p, 2 * m, w))), ((8, 128), F32, self.full((8, 128)))],
        )
        return both, swap(both, 1)

    def whole(self, c, got):
        p, n, m, w = self.p, self.n, self.m, self.w

        def body(where, mine, came, out, block, sems):
            z = where[1]
            for src, at, k in ((mine, 0, 0), (mine, m, 3), (came, 0, 1), (came, m, 2)):
                block[:, ds(z ^ k, m)] = src[:, at : at + m]
            move((block, out.at[self.of_out(where, c, 0, 0, p)], sems.at[0]))

        self.out, block = self.call(
            body,
            [(a, self.full((p, 2 * m, w))) for a in got],
            [((self.projs, NY * n, w), BF16, HBM), ((p, n, w), BF16, self.full((p, n, w)))],
            alias=[(self.out, 0)],
            scratch=[pltpu.SemaphoreType.DMA((1,))],
        )
        return shift(block, 1), shift(block, -1)

    def pass_on(self, c, got):
        p, h, n, w = self.p, self.h, self.n, self.w
        many = len(got) // 2

        def body(where, *refs):
            came, (out, up, down, sems) = refs[: 2 * many], refs[2 * many :]
            copies = []
            for j in range(many):
                below, above = came[2 * j], came[2 * j + 1]
                copies += [
                    (below.at[pl.ds(0, h)], up.at[pl.ds(j * h, h)], sems.at[4 * j]),
                    (above.at[pl.ds(h, h)], down.at[pl.ds(j * h, h)], sems.at[4 * j + 1]),
                    (below, out.at[self.of_out(where, c + j, 3, 0, p)], sems.at[4 * j + 2]),
                    (above, out.at[self.of_out(where, c + j, 1, 0, p)], sems.at[4 * j + 3]),
                ]
            move(*copies)

        self.out, up, down = self.call(
            body,
            [(a, ANY) for a in got],
            [(self.out.shape, BF16, HBM)] + [((many * h, n, w), BF16, ANY)] * 2,
            alias=[(self.out, 0)],
            scratch=[pltpu.SemaphoreType.DMA((4 * many,))],
        )
        return shift(up, 1), shift(down, -1)

    def finish(self, c, got):
        h = self.h
        many = got[0].shape[0] // h

        def body(where, low, high, out, sems):
            copies = []
            for j in range(many):
                r = pl.ds(j * h, h)
                copies += [
                    (low.at[r], out.at[self.of_out(where, c + j, 2, 0, h)], sems.at[2 * j]),
                    (high.at[r], out.at[self.of_out(where, c + j, 2, h, h)], sems.at[2 * j + 1]),
                ]
            move(*copies)

        (self.out,) = self.call(
            body,
            [(a, ANY) for a in got],
            [(self.out.shape, BF16, HBM)],
            alias=[(self.out, 0)],
            scratch=[pltpu.SemaphoreType.DMA((2 * many,))],
        )


PLAN = (
    "a0", "a12", "m0", "m1", "m2", "s0", "h0", "s1", "u0", "a3",
    "h1", "s2", "p0", "m3", "u1", "h2", "p1", "g0", "u2", "s3",
    "g1", "p2", "h3", "o0", "u3", "o1", "f0", "g2", "p3", "f1",
    "g3", "o2", "o3", "f2", "f3",
)


def on_device(x, master, momentum):
    where = jnp.stack([lax.axis_index("y"), lax.axis_index("z")]).astype(jnp.int32)
    s = Steps(x, master, momentum, where)
    held = {}
    stages = dict(h=s.fourth, u=s.update, p=s.pair, g=s.whole, f=s.finish)
    for step in PLAN:
        kind, c, last = step[0], int(step[1]), int(step[-1])
        chunks = range(c, last + 1)
        if kind == "a":
            got = s.first(c, len(chunks))
        elif kind == "m":
            got = s.second(c, len(chunks), *held[c])
        elif kind == "s":
            got = s.third(c, *held[c])
        elif kind == "o":
            got = s.pass_on(c, sum((held[e] for e in chunks), ()))
        else:
            got = stages[kind](c, held[c])
        for j, e in enumerate(chunks):
            held[e] = (got, j) if kind in "am" else got
    join = lambda d: jnp.concatenate([d[c] for c in range(CHUNKS)])
    return s.out, join(s.new_master), join(s.new_momentum)


def solution(mesh):
    fine = Mesh(mesh.devices.reshape(NY, NZ, -1), ("y", "z", "fsdp"))
    owned = P(None, ("fsdp", "y", "z"), None)
    return jax.shard_map(
        on_device,
        mesh=fine,
        in_specs=(P(("y", "z"), None, "fsdp", None), owned, owned),
        out_specs=(P(None, "fsdp", None), owned, owned),
        check_vma=False,
    )
```

```python
import functools

import jax
import jax.numpy as jnp
from jax import lax
from jax.experimental import pallas as pl
from jax.experimental.pallas import tpu as pltpu
from jax.sharding import Mesh, PartitionSpec as P

RATE = 0.7
MU = 0.9
NY = 4
NZ = 4
CHUNKS = 4
F32 = jnp.float32
BF16 = jnp.bfloat16
ANY = pl.BlockSpec(memory_space=pl.ANY)
HBM = pl.BlockSpec(memory_space=pltpu.HBM)
ROWS = 32
VMEM = 16 << 20


def shift(a, s):
    return lax.ppermute(a, "y", [(i, (i + s) % NY) for i in range(NY)])


def swap(a, k):
    return lax.ppermute(a, "z", [(i, i ^ k) for i in range(NZ)])


def ds(block, n):
    return pl.ds(pl.multiple_of(block * n, n), n)


def move(*copies):
    started = [pltpu.make_async_copy(*c) for c in copies]
    for c in started:
        c.start()
    for c in started:
        c.wait()


class Steps:
    def __init__(self, x, master, momentum, where):
        self.x, self.master, self.momentum, self.where = x, master, momentum, where
        _, self.projs, rows, self.w = x.shape
        self.p = self.projs // CHUNKS
        self.h = self.p // 2
        self.n = rows // NY
        self.m = self.n // NZ
        self.last = None
        self.out, self.new_master, self.new_momentum = None, {}, {}

    def call(self, body, ins, outs, alias=(), scratch=()):
        arrays = [a for a, _ in ins]
        specs = [s for _, s in ins]
        n_in, n_out = len(arrays), len(outs)
        aliases = {}
        for array, k in alias:
            if array is not None:
                aliases[1 + len(arrays)] = k
                arrays.append(array)
                specs.append(outs[k][2])
        if self.last is not None:
            arrays.append(self.last)
            specs.append(ANY)
        total = len(arrays)

        def kernel(where, *refs):
            body(where, *refs[:n_in], *refs[total:])

        got = pl.pallas_call(
            kernel,
            out_shape=[jax.ShapeDtypeStruct(s, t) for s, t, _ in outs],
            grid_spec=pltpu.PrefetchScalarGridSpec(
                num_scalar_prefetch=1,
                grid=(1,),
                in_specs=specs,
                out_specs=[s for _, _, s in outs],
                scratch_shapes=scratch,
            ),
            input_output_aliases=aliases,
            compiler_params=pltpu.CompilerParams(vmem_limit_bytes=VMEM),
            cost_estimate=pl.CostEstimate(flops=1000, bytes_accessed=1000, transcendentals=0),
        )(self.where, *arrays)
        if len(got) > 1:
            self.last = got[-1]
        return got

    def full(self, shape):
        return pl.BlockSpec(shape, lambda i, w: (0,) * len(shape))

    def of_x(self, where, c, d, first, count):
        return (0, pl.ds(c * self.p + first, count), ds((where[0] + d) % NY, self.n))

    def of_out(self, where, c, d, first, count):
        return (pl.ds(c * self.p + first, count), ds((where[0] + d) % NY, self.n))

    def first(self, c, many):
        p, h, n, w = self.p, self.h, self.n, self.w
        if self.last is None:
            block = (self.where[0] + 2) % NY * n
            far = [lax.dynamic_slice(self.x, (0, (c + j) * p, block, 0), (1, p, n, w))[0] for j in range(many)]
            self.last = up = jnp.concatenate([t[h:] for t in far])
            return shift(up, 1), shift(jnp.concatenate([t[:h] for t in far]), -1)

        def body(where, x, up, down, sems):
            copies = []
            for j in range(many):
                r = pl.ds(j * h, h)
                copies += [
                    (x.at[self.of_x(where, c + j, 2, h, h)], up.at[r], sems.at[2 * j]),
                    (x.at[self.of_x(where, c + j, 2, 0, h)], down.at[r], sems.at[2 * j + 1]),
                ]
            move(*copies)

        up, down = self.call(
            body,
            [(self.x, HBM)],
            [((many * h, n, w), BF16, ANY)] * 2,
            scratch=[pltpu.SemaphoreType.DMA((2 * many,))],
        )
        return shift(up, 1), shift(down, -1)

    def second(self, c, many, got, j):
        p, h, n, w = self.p, self.h, self.n, self.w
        part = pl.BlockSpec((many * h, n, w), lambda i, w_: (j // many, 0, 0))

        def body(where, x, below, above, up, down, sems):
            move(
                (x.at[self.of_x(where, c, 1, 0, many * p)], up, sems.at[0]),
                (x.at[self.of_x(where, c, 3, 0, many * p)], down, sems.at[1]),
            )

            @pl.loop(0, n // ROWS)
            def _(i):
                r = ds(i, ROWS)
                for k in range(many):
                    came, low, high = pl.ds(k * h, h), pl.ds(k * p, h), pl.ds(k * p + h, h)
                    up[high, r] = (up[high, r].astype(F32) + below[came, r].astype(F32)).astype(BF16)
                    down[low, r] = (down[low, r].astype(F32) + above[came, r].astype(F32)).astype(BF16)

        up, down = self.call(
            body,
            [(self.x, HBM), (got[0], part), (got[1], part)],
            [((many * p, n, w), BF16, self.full((many * p, n, w)))] * 2,
            scratch=[pltpu.SemaphoreType.DMA((2,))],
        )
        return shift(up, 1), shift(down, -1)

    def third(self, c, got, j):
        p, n, m, w = self.p, self.n, self.m, self.w
        part = pl.BlockSpec((p, n, w), lambda i, w_: (j, 0, 0))

        def body(where, x, below, above, keep, send, own, sems):
            move((x.at[self.of_x(where, c, 0, 0, p)], own, sems.at[0]))
            z = where[1]
            for out, at, k in ((keep, 0, 0), (keep, m, 3), (send, 0, 1), (send, m, 2)):
                r = ds(z ^ k, m)
                t = own[:, r].astype(F32) + below[:, r].astype(F32) + above[:, r].astype(F32)
                out[:, at : at + m] = t.astype(out.dtype)

        keep, send = self.call(
            body,
            [(self.x, HBM), (got[0], part), (got[1], part)],
            [
                ((p, 2 * m, w), F32, self.full((p, 2 * m, w))),
                ((p, 2 * m, w), BF16, self.full((p, 2 * m, w))),
            ],
            scratch=[pltpu.VMEM((p, n, w), BF16), pltpu.SemaphoreType.DMA((1,))],
        )
        return keep, swap(send, 1)

    def fourth(self, c, got):
        p, m, w = self.p, self.m, self.w

        def body(where, kept, came, keep, send):
            keep[...] = kept[:, :m] + came[:, :m].astype(F32)
            send[...] = (kept[:, m:] + came[:, m:].astype(F32)).astype(BF16)

        keep, send = self.call(
            body,
            [(a, self.full((p, 2 * m, w))) for a in got],
            [((p, m, w), F32, self.full((p, m, w))), ((p, m, w), BF16, self.full((p, m, w)))],
        )
        return keep, swap(send, 3)

    def update(self, c, got):
        p, m, w = self.p, self.m, self.w
        mine = pl.BlockSpec((p, m, w), lambda i, w_: (c, 0, 0))

        def body(where, kept, came, master, momentum, new_master, new_momentum, fresh):
            pseudo = master[...] - (kept[...] + came[...].astype(F32)) / 16
            nv = MU * momentum[...] + pseudo
            nm = master[...] - RATE * (pseudo + MU * nv)
            new_master[...] = nm
            new_momentum[...] = nv
            fresh[...] = nm.astype(BF16)

        nm, nv, fresh = self.call(
            body,
            [(a, self.full((p, m, w))) for a in got] + [(self.master, mine), (self.momentum, mine)],
            [
                ((p, m, w), F32, self.full((p, m, w))),
                ((p, m, w), F32, self.full((p, m, w))),
                ((p, m, w), BF16, self.full((p, m, w))),
            ],
        )
        self.new_master[c], self.new_momentum[c] = nm, nv
        return fresh, swap(fresh, 3)

    def pair(self, c, got):
        p, m, w = self.p, self.m, self.w

        def body(where, mine, came, both, mark):
            both[:, :m] = mine[...]
            both[:, m:] = came[...]

        both, _ = self.call(
            body,
            [(a, self.full((p, m, w))) for a in got],
            [((p, 2 * m, w), BF16, self.full((p, 2 * m, w))), ((8, 128), F32, self.full((8, 128)))],
        )
        return both, swap(both, 1)

    def whole(self, c, got):
        p, n, m, w = self.p, self.n, self.m, self.w

        def body(where, mine, came, out, block, sems):
            z = where[1]
            for src, at, k in ((mine, 0, 0), (mine, m, 3), (came, 0, 1), (came, m, 2)):
                block[:, ds(z ^ k, m)] = src[:, at : at + m]
            move((block, out.at[self.of_out(where, c, 0, 0, p)], sems.at[0]))

        self.out, block = self.call(
            body,
            [(a, self.full((p, 2 * m, w))) for a in got],
            [((self.projs, NY * n, w), BF16, HBM), ((p, n, w), BF16, self.full((p, n, w)))],
            alias=[(self.out, 0)],
            scratch=[pltpu.SemaphoreType.DMA((1,))],
        )
        return shift(block, 1), shift(block, -1)

    def pass_on(self, c, got):
        p, h, n, w = self.p, self.h, self.n, self.w
        many = len(got) // 2

        def body(where, *refs):
            came, (out, up, down, sems) = refs[: 2 * many], refs[2 * many :]
            copies = []
            for j in range(many):
                below, above = came[2 * j], came[2 * j + 1]
                copies += [
                    (below.at[pl.ds(0, h)], up.at[pl.ds(j * h, h)], sems.at[4 * j]),
                    (above.at[pl.ds(h, h)], down.at[pl.ds(j * h, h)], sems.at[4 * j + 1]),
                    (below, out.at[self.of_out(where, c + j, 3, 0, p)], sems.at[4 * j + 2]),
                    (above, out.at[self.of_out(where, c + j, 1, 0, p)], sems.at[4 * j + 3]),
                ]
            move(*copies)

        self.out, up, down = self.call(
            body,
            [(a, ANY) for a in got],
            [(self.out.shape, BF16, HBM)] + [((many * h, n, w), BF16, ANY)] * 2,
            alias=[(self.out, 0)],
            scratch=[pltpu.SemaphoreType.DMA((4 * many,))],
        )
        return shift(up, 1), shift(down, -1)

    def finish(self, c, got):
        h = self.h
        many = got[0].shape[0] // h

        def body(where, low, high, out, sems):
            copies = []
            for j in range(many):
                r = pl.ds(j * h, h)
                copies += [
                    (low.at[r], out.at[self.of_out(where, c + j, 2, 0, h)], sems.at[2 * j]),
                    (high.at[r], out.at[self.of_out(where, c + j, 2, h, h)], sems.at[2 * j + 1]),
                ]
            move(*copies)

        (self.out,) = self.call(
            body,
            [(a, ANY) for a in got],
            [(self.out.shape, BF16, HBM)],
            alias=[(self.out, 0)],
            scratch=[pltpu.SemaphoreType.DMA((2 * many,))],
        )


PLAN = (
    "a0", "a12", "m0", "m1", "m2", "s0", "h0", "s1", "u0", "a3",
    "h1", "s2", "m3", "p0", "u1", "h2", "g0", "p1", "u2", "s3",
    "g1", "p2", "h3", "o0", "u3", "o1", "f0", "g2", "p3", "f1",
    "g3", "o2", "o3", "f2", "f3",
)


def on_device(x, master, momentum):
    where = jnp.stack([lax.axis_index("y"), lax.axis_index("z")]).astype(jnp.int32)
    s = Steps(x, master, momentum, where)
    held = {}
    stages = dict(h=s.fourth, u=s.update, p=s.pair, g=s.whole, f=s.finish)
    for step in PLAN:
        kind, c, last = step[0], int(step[1]), int(step[-1])
        chunks = range(c, last + 1)
        if kind == "a":
            got = s.first(c, len(chunks))
        elif kind == "m":
            got = s.second(c, len(chunks), *held[c])
        elif kind == "s":
            got = s.third(c, *held[c])
        elif kind == "o":
            got = s.pass_on(c, sum((held[e] for e in chunks), ()))
        else:
            got = stages[kind](c, held[c])
        for j, e in enumerate(chunks):
            held[e] = (got, j) if kind in "am" else got
    join = lambda d: jnp.concatenate([d[c] for c in range(CHUNKS)])
    return s.out, join(s.new_master), join(s.new_momentum)


def solution(mesh):
    fine = Mesh(mesh.devices.reshape(NY, NZ, -1), ("y", "z", "fsdp"))
    owned = P(None, ("fsdp", "y", "z"), None)
    return jax.shard_map(
        on_device,
        mesh=fine,
        in_specs=(P(("y", "z"), None, "fsdp", None), owned, owned),
        out_specs=(P(None, "fsdp", None), owned, owned),
        check_vma=False,
    )
```

```python
import functools

import jax
import jax.numpy as jnp
from jax import lax
from jax.experimental import pallas as pl
from jax.experimental.pallas import tpu as pltpu
from jax.sharding import Mesh, PartitionSpec as P

RATE = 0.7
MU = 0.9
NY = 4
NZ = 4
CHUNKS = 4
F32 = jnp.float32
BF16 = jnp.bfloat16
ANY = pl.BlockSpec(memory_space=pl.ANY)
HBM = pl.BlockSpec(memory_space=pltpu.HBM)
ROWS = 32
VMEM = 16 << 20


def shift(a, s):
    return lax.ppermute(a, "y", [(i, (i + s) % NY) for i in range(NY)])


def swap(a, k):
    return lax.ppermute(a, "z", [(i, i ^ k) for i in range(NZ)])


def ds(block, n):
    return pl.ds(pl.multiple_of(block * n, n), n)


def move(*copies):
    started = [pltpu.make_async_copy(*c) for c in copies]
    for c in started:
        c.start()
    for c in started:
        c.wait()


class Steps:
    def __init__(self, x, master, momentum, where):
        self.x, self.master, self.momentum, self.where = x, master, momentum, where
        _, self.projs, rows, self.w = x.shape
        self.p = self.projs // CHUNKS
        self.h = self.p // 2
        self.n = rows // NY
        self.m = self.n // NZ
        self.last = None
        self.out, self.new_master, self.new_momentum, self.block = None, {}, {}, {}

    def call(self, body, ins, outs, alias=(), scratch=()):
        arrays = [a for a, _ in ins]
        specs = [s for _, s in ins]
        n_in, n_out = len(arrays), len(outs)
        aliases = {}
        for array, k in alias:
            if array is not None:
                aliases[1 + len(arrays)] = k
                arrays.append(array)
                specs.append(outs[k][2])
        if self.last is not None:
            arrays.append(self.last)
            specs.append(ANY)
        total = len(arrays)

        def kernel(where, *refs):
            body(where, *refs[:n_in], *refs[total:])

        got = pl.pallas_call(
            kernel,
            out_shape=[jax.ShapeDtypeStruct(s, t) for s, t, _ in outs],
            grid_spec=pltpu.PrefetchScalarGridSpec(
                num_scalar_prefetch=1,
                grid=(1,),
                in_specs=specs,
                out_specs=[s for _, _, s in outs],
                scratch_shapes=scratch,
            ),
            input_output_aliases=aliases,
            compiler_params=pltpu.CompilerParams(vmem_limit_bytes=VMEM),
            cost_estimate=pl.CostEstimate(flops=1000, bytes_accessed=1000, transcendentals=0),
        )(self.where, *arrays)
        if len(got) > 1:
            self.last = got[-1]
        return got

    def full(self, shape):
        return pl.BlockSpec(shape, lambda i, w: (0,) * len(shape))

    def of_x(self, where, c, d, first, count):
        return (0, pl.ds(c * self.p + first, count), ds((where[0] + d) % NY, self.n))

    def of_out(self, where, c, d, first, count):
        return (pl.ds(c * self.p + first, count), ds((where[0] + d) % NY, self.n))

    def first(self, c, many):
        p, h, n, w = self.p, self.h, self.n, self.w
        if self.last is None:
            block = (self.where[0] + 2) % NY * n
            far = [lax.dynamic_slice(self.x, (0, (c + j) * p, block, 0), (1, p, n, w))[0] for j in range(many)]
            self.last = up = jnp.concatenate([t[h:] for t in far])
            return shift(up, 1), shift(jnp.concatenate([t[:h] for t in far]), -1)

        def body(where, x, up, down, sems):
            copies = []
            for j in range(many):
                r = pl.ds(j * h, h)
                copies += [
                    (x.at[self.of_x(where, c + j, 2, h, h)], up.at[r], sems.at[2 * j]),
                    (x.at[self.of_x(where, c + j, 2, 0, h)], down.at[r], sems.at[2 * j + 1]),
                ]
            move(*copies)

        up, down = self.call(
            body,
            [(self.x, HBM)],
            [((many * h, n, w), BF16, ANY)] * 2,
            scratch=[pltpu.SemaphoreType.DMA((2 * many,))],
        )
        return shift(up, 1), shift(down, -1)

    def second(self, c, many, got, j):
        p, h, n, w = self.p, self.h, self.n, self.w
        part = pl.BlockSpec((many * h, n, w), lambda i, w_: (j // many, 0, 0))

        def body(where, x, below, above, up, down, sems):
            move(
                (x.at[self.of_x(where, c, 1, 0, many * p)], up, sems.at[0]),
                (x.at[self.of_x(where, c, 3, 0, many * p)], down, sems.at[1]),
            )

            @pl.loop(0, n // ROWS)
            def _(i):
                r = ds(i, ROWS)
                for k in range(many):
                    came, low, high = pl.ds(k * h, h), pl.ds(k * p, h), pl.ds(k * p + h, h)
                    up[high, r] = (up[high, r].astype(F32) + below[came, r].astype(F32)).astype(BF16)
                    down[low, r] = (down[low, r].astype(F32) + above[came, r].astype(F32)).astype(BF16)

        up, down = self.call(
            body,
            [(self.x, HBM), (got[0], part), (got[1], part)],
            [((many * p, n, w), BF16, self.full((many * p, n, w)))] * 2,
            scratch=[pltpu.SemaphoreType.DMA((2,))],
        )
        return shift(up, 1), shift(down, -1)

    def third(self, c, got, j):
        p, n, m, w = self.p, self.n, self.m, self.w
        part = pl.BlockSpec((p, n, w), lambda i, w_: (j, 0, 0))

        def body(where, x, below, above, keep, send, own, sems):
            move((x.at[self.of_x(where, c, 0, 0, p)], own, sems.at[0]))
            z = where[1]
            for out, at, k in ((keep, 0, 0), (keep, m, 3), (send, 0, 1), (send, m, 2)):
                r = ds(z ^ k, m)
                t = own[:, r].astype(F32) + below[:, r].astype(F32) + above[:, r].astype(F32)
                out[:, at : at + m] = t.astype(out.dtype)

        keep, send = self.call(
            body,
            [(self.x, HBM), (got[0], part), (got[1], part)],
            [
                ((p, 2 * m, w), F32, self.full((p, 2 * m, w))),
                ((p, 2 * m, w), BF16, self.full((p, 2 * m, w))),
            ],
            scratch=[pltpu.VMEM((p, n, w), BF16), pltpu.SemaphoreType.DMA((1,))],
        )
        return keep, swap(send, 1)

    def fourth(self, c, got):
        p, m, w = self.p, self.m, self.w

        def body(where, kept, came, keep, send):
            keep[...] = kept[:, :m] + came[:, :m].astype(F32)
            send[...] = (kept[:, m:] + came[:, m:].astype(F32)).astype(BF16)

        keep, send = self.call(
            body,
            [(a, self.full((p, 2 * m, w))) for a in got],
            [((p, m, w), F32, self.full((p, m, w))), ((p, m, w), BF16, self.full((p, m, w)))],
        )
        return keep, swap(send, 3)

    def update(self, c, got):
        p, m, w = self.p, self.m, self.w
        mine = pl.BlockSpec((p, m, w), lambda i, w_: (c, 0, 0))

        def body(where, kept, came, master, momentum, new_master, new_momentum, fresh):
            pseudo = master[...] - (kept[...] + came[...].astype(F32)) / 16
            nv = MU * momentum[...] + pseudo
            nm = master[...] - RATE * (pseudo + MU * nv)
            new_master[...] = nm
            new_momentum[...] = nv
            fresh[...] = nm.astype(BF16)

        nm, nv, fresh = self.call(
            body,
            [(a, self.full((p, m, w))) for a in got] + [(self.master, mine), (self.momentum, mine)],
            [
                ((p, m, w), F32, self.full((p, m, w))),
                ((p, m, w), F32, self.full((p, m, w))),
                ((p, m, w), BF16, self.full((p, m, w))),
            ],
        )
        self.new_master[c], self.new_momentum[c] = nm, nv
        return fresh, swap(fresh, 3)

    def pair(self, c, got):
        p, m, w = self.p, self.m, self.w

        def body(where, mine, came, both, mark):
            both[:, :m] = mine[...]
            both[:, m:] = came[...]

        both, _ = self.call(
            body,
            [(a, self.full((p, m, w))) for a in got],
            [((p, 2 * m, w), BF16, self.full((p, 2 * m, w))), ((8, 128), F32, self.full((8, 128)))],
        )
        return both, swap(both, 1)

    def whole(self, c, got):
        p, n, m, w = self.p, self.n, self.m, self.w

        def body(where, mine, came, block, mark):
            z = where[1]
            for src, at, k in ((mine, 0, 0), (mine, m, 3), (came, 0, 1), (came, m, 2)):
                block[:, ds(z ^ k, m)] = src[:, at : at + m]

        block, _ = self.call(
            body,
            [(a, self.full((p, 2 * m, w))) for a in got],
            [((p, n, w), BF16, self.full((p, n, w))), ((8, 128), F32, self.full((8, 128)))],
        )
        self.block[c] = block
        return shift(block, 1), shift(block, -1)

    def blocks_out(self, where, c, refs, out, sems, at):
        return [
            (ref, out.at[self.of_out(where, c, d, 0, self.p)], sems.at[at + k])
            for k, (ref, d) in enumerate(zip(refs, (0, 3, 1)))
        ]

    def pass_on(self, c, got):
        p, h, n, w = self.p, self.h, self.n, self.w
        late = c == CHUNKS - 1
        blocks = (self.block[c],) + tuple(got)
        if late:
            self.late = blocks

        def body(where, *refs):
            (_, below, above), (up, down, sems) = refs[:3], refs[-3:]
            copies = [
                (below.at[pl.ds(0, h)], up, sems.at[0]),
                (above.at[pl.ds(h, h)], down, sems.at[1]),
            ]
            if not late:
                copies += self.blocks_out(where, c, refs[:3], refs[3], sems, 2)
            move(*copies)

        outs = [((h, n, w), BF16, ANY)] * 2
        if not late:
            outs = [((self.projs, NY * n, w), BF16, HBM)] + outs
        made = self.call(
            body,
            [(a, ANY) for a in blocks],
            outs,
            alias=[] if late else [(self.out, 0)],
            scratch=[pltpu.SemaphoreType.DMA((5,))],
        )
        if not late:
            self.out = made[0]
        return shift(made[-2], 1), shift(made[-1], -1)

    def finish(self, c, got):
        h = self.h
        more = self.late if c == CHUNKS - 2 else ()

        def body(where, low, high, *refs):
            out, sems = refs[-2:]
            copies = [
                (low, out.at[self.of_out(where, c, 2, 0, h)], sems.at[0]),
                (high, out.at[self.of_out(where, c, 2, h, h)], sems.at[1]),
            ]
            if more:
                copies += self.blocks_out(where, c + 1, refs[:3], out, sems, 2)
            move(*copies)

        (self.out,) = self.call(
            body,
            [(a, ANY) for a in tuple(got) + more],
            [(self.out.shape, BF16, HBM)],
            alias=[(self.out, 0)],
            scratch=[pltpu.SemaphoreType.DMA((5,))],
        )


PLAN = (
    "a0", "a12", "m0", "m1", "m2", "s0", "h0", "s1", "u0", "a3",
    "h1", "s2", "p0", "m3", "u1", "h2", "p1", "g0", "u2", "s3",
    "g1", "p2", "h3", "o0", "u3", "o1", "f0", "g2", "p3", "f1",
    "g3", "o2", "o3", "f2", "f3",
)


def on_device(x, master, momentum):
    where = jnp.stack([lax.axis_index("y"), lax.axis_index("z")]).astype(jnp.int32)
    s = Steps(x, master, momentum, where)
    held = {}
    stages = dict(h=s.fourth, u=s.update, p=s.pair, g=s.whole, f=s.finish)
    for step in PLAN:
        kind, c, last = step[0], int(step[1]), int(step[-1])
        chunks = range(c, last + 1)
        if kind == "a":
            got = s.first(c, len(chunks))
        elif kind == "m":
            got = s.second(c, len(chunks), *held[c])
        elif kind == "s":
            got = s.third(c, *held[c])
        elif kind == "o":
            got = s.pass_on(c, held[c])
        else:
            got = stages[kind](c, held[c])
        for j, e in enumerate(chunks):
            held[e] = (got, j) if kind in "am" else got
    join = lambda d: jnp.concatenate([d[c] for c in range(CHUNKS)])
    return s.out, join(s.new_master), join(s.new_momentum)


def solution(mesh):
    fine = Mesh(mesh.devices.reshape(NY, NZ, -1), ("y", "z", "fsdp"))
    owned = P(None, ("fsdp", "y", "z"), None)
    return jax.shard_map(
        on_device,
        mesh=fine,
        in_specs=(P(("y", "z"), None, "fsdp", None), owned, owned),
        out_specs=(P(None, "fsdp", None), owned, owned),
        check_vma=False,
    )
```
